32 devices in a mesh: ctx: 8 (over z, x), ch: 4 (over y, core).
Axes of the slice: x: 2, y: 2, z: 4, core: 2. Of those that a mesh axis runs over, the one named last changes fastest.
Arguments:
- x_slab: bfloat16 [8192, 1024], P('ch', 'ctx'), may hold values from -6 to 6
- filter_taps: float32 [128, 1024], P('ch', 'ctx'), may hold values from -0.1875 to 0.1875
- mix_weight: bfloat16 [8192, 3, 128], P('ch'), may hold values from -0.0625 to 0.0625
- skip_gain: float32 [128], P('ch'), may hold values from 0.25 to 1.5
- cotangent: bfloat16 [128, 1024], P('ch', 'ctx'), may hold values from -6 to 6
Outputs:
- input_grad: bfloat16 [8192, 1024], P('ch', 'ctx')
- weight_grad: float32 [8192, 3, 128], P(('ch', 'ctx'))
- filter_grad: float32 [128, 1024], P('ch', 'ctx')
The draws below stay inside these ranges and needn't reach their ends.
All inputs are finite; a program needn't handle non-finite values.
Results may differ from the reference program's by a relative error of at most 0.005.
Values may be sent and summed in bfloat16 or wider, within the bound.
A program may use at most 64 MiB of HBM per device.

```python
import jax
import jax.numpy as jnp
from jax import lax

MODEL_WIDTH = 8192
CHANNELS = 128
LENGTH = 1024


def raised(drawn, rng, source, target, parts, factor):
    owner, partner = [(jnp.arange(drawn.shape[dim]) // (drawn.shape[dim] // parts)).reshape([-1 if axis == dim else 1 for axis in range(drawn.ndim)]) for dim in (source, target)]
    chosen = jax.random.permutation(rng, parts)[partner]
    strong = (owner == chosen) | (owner == (partner + parts // 2) % parts)
    return jnp.where(strong, factor * drawn, drawn)


def block_scale(stream_key, extent, shards, least, top_value):
    factor_of, own = 1.0, jax.random.fold_in(stream_key, 6)
    for position, blocks in shards:
        steps = jnp.exp(jax.random.uniform(jax.random.fold_in(own, position), (blocks,), jnp.float32, least / len(shards), top_value / len(shards)))
        factor_of = factor_of * jnp.repeat(steps, extent[position] // blocks).reshape([-1 if axis == position else 1 for axis in range(len(extent))])
    return factor_of


def noise(rng, dims, scale, reach, cuts=(), kind=jnp.bfloat16):
    drawn = scale * jax.random.normal(rng, dims, jnp.float32)
    if cuts:
        drawn = drawn * block_scale(rng, dims, cuts, -0.22, 0.18)
    return jnp.clip(drawn, -reach, reach).astype(kind)


def bell_draw_with(stream_key, extent, deviation, limit, pieces, heavy, dtype=jnp.bfloat16):
    result = deviation * jax.random.normal(stream_key, extent, jnp.float32)
    if pieces:
        result = result * block_scale(stream_key, extent, pieces, -0.22, 0.18)
    return jnp.clip(raised(result, jax.random.fold_in(stream_key, 3), *heavy), -limit, limit).astype(dtype)


def setup_inputs(seed: int = 0) -> dict:
    arg_keys = jax.random.split(jax.random.key(seed), 6)
    return {
        "x_slab": bell_draw_with(arg_keys[0], (MODEL_WIDTH, LENGTH), 1.0, 6.0, ((0, 4), (1, 8)), (1, 0, 8, 2.0)),
        "filter_taps": noise(arg_keys[1], (CHANNELS, LENGTH), LENGTH ** -0.5, 0.1875, ((0, 4), (1, 8)), jnp.float32),
        "mix_weight": noise(arg_keys[2], (MODEL_WIDTH, 3, CHANNELS), MODEL_WIDTH ** -0.5, 0.0625, ((0, 4),)),
        "skip_gain": jnp.clip(0.25 + 1.25 * jax.random.uniform(arg_keys[3], (CHANNELS,), jnp.float32) ** block_scale(arg_keys[3], (CHANNELS,), ((0, 4),), -0.2, 0.2), 0.25, 1.5),
        "cotangent": noise(arg_keys[4], (CHANNELS, LENGTH), 1.0, 6.0, ((0, 4), (1, 8))),
    }


def reference(x_slab, filter_taps, mix_weight, skip_gain, cotangent):
    inputs = x_slab.astype(jnp.float32)
    weights = mix_weight.astype(jnp.float32)
    projected = jnp.einsum('ijo,il->jol', weights, inputs, precision=lax.Precision.HIGHEST)
    outer_gate = projected[0]
    inner_gate = projected[1]
    values_in = projected[2]
    product = inner_gate * values_in
    points = 2 * LENGTH
    prod_spec = jnp.fft.rfft(product, n=points, axis=1)
    filt_spec = jnp.fft.rfft(filter_taps, n=points, axis=1)
    convolved = jnp.fft.irfft(prod_spec * filt_spec, n=points, axis=1)[:, :LENGTH]
    gain = skip_gain[:, None]
    mixed = convolved + gain * product
    grad_out = cotangent.astype(jnp.float32)
    grad_mixed = grad_out * outer_gate
    grad_outer = grad_out * mixed
    grad_spec = jnp.fft.rfft(grad_mixed, n=points, axis=1)
    grad_product = jnp.fft.irfft(grad_spec * jnp.conj(filt_spec), n=points, axis=1)[:, :LENGTH] + gain * grad_mixed
    scale = 1.0 / jnp.sqrt(jnp.float32(LENGTH))
    filter_grad = jnp.fft.irfft(grad_spec * jnp.conj(prod_spec), n=points, axis=1)[:, :LENGTH] * scale
    grad_proj = jnp.stack([grad_outer, grad_product * values_in, grad_product * inner_gate]).astype(jnp.bfloat16)
    grad_wide = grad_proj.astype(jnp.float32)
    weight_grad = jnp.einsum('il,jol->ijo', inputs, grad_wide, precision=lax.Precision.HIGHEST) * scale
    input_grad = jnp.einsum('ijo,jol->il', weights, grad_wide, precision=lax.Precision.HIGHEST).astype(jnp.bfloat16)
    return (input_grad, weight_grad, filter_grad)
```

```python
import functools
import math

import jax
import jax.numpy as jnp
from jax import lax
from jax.experimental import pallas as pl
from jax.experimental.pallas import tpu as pltpu
from jax.sharding import PartitionSpec as P

highest = lax.Precision.HIGHEST


def angle_table(rows, cols, period):
    product = (
        jnp.arange(rows, dtype=jnp.int32)[:, None]
        * jnp.arange(cols, dtype=jnp.int32)[None, :]
        % period
    )
    phase = product.astype(jnp.float32) * (2.0 * math.pi / period)
    return (jnp.cos(phase), jnp.sin(phase))


def twiddle(count, width):
    span = width // count
    places = lax.axis_index("ctx") * span + jnp.arange(span, dtype=jnp.int32)
    total = 2 * count * width
    product = jnp.arange(2 * count, dtype=jnp.int32)[:, None] * places[None, :] % total
    phase = product.astype(jnp.float32) * (2.0 * math.pi / total)
    return (jnp.cos(phase), jnp.sin(phase))


def spread(fields):
    return lax.all_to_all(fields[:, None, :], "ctx", split_axis=2, concat_axis=1, tiled=True)


def gather_back(parted):
    joined = lax.all_to_all(parted, "ctx", split_axis=1, concat_axis=2, tiled=True)
    return joined[:, 0, :]


def spectrum(parted):
    count = parted.shape[1]
    width = count * parted.shape[2]
    cos_j, sin_j = angle_table(count, 2 * count, 2 * count)
    real_part = jnp.einsum("rjs,jk->rks", parted, cos_j, precision=highest)
    imag_part = -jnp.einsum("rjs,jk->rks", parted, sin_j, precision=highest)
    cos_t, sin_t = twiddle(count, width)
    turned = jnp.stack(
        [real_part * cos_t + imag_part * sin_t, imag_part * cos_t - real_part * sin_t]
    )
    moved = lax.all_to_all(turned, "ctx", split_axis=2, concat_axis=3, tiled=True)
    cos_b, sin_b = angle_table(width, width, width)
    real_out = jnp.einsum("rkb,bm->rkm", moved[0], cos_b, precision=highest) + jnp.einsum(
        "rkb,bm->rkm", moved[1], sin_b, precision=highest
    )
    imag_out = jnp.einsum("rkb,bm->rkm", moved[1], cos_b, precision=highest) - jnp.einsum(
        "rkb,bm->rkm", moved[0], sin_b, precision=highest
    )
    return jnp.stack([real_out, imag_out])


def unspectrum(spec):
    count = lax.axis_size("ctx")
    width = spec.shape[3]
    cos_b, sin_b = angle_table(width, width, width)
    real_part = jnp.einsum("rkm,mb->rkb", spec[0], cos_b, precision=highest) - jnp.einsum(
        "rkm,mb->rkb", spec[1], sin_b, precision=highest
    )
    imag_part = jnp.einsum("rkm,mb->rkb", spec[1], cos_b, precision=highest) + jnp.einsum(
        "rkm,mb->rkb", spec[0], sin_b, precision=highest
    )
    moved = lax.all_to_all(
        jnp.stack([real_part, imag_part]), "ctx", split_axis=3, concat_axis=2, tiled=True
    )
    cos_t, sin_t = twiddle(count, width)
    real_turn = moved[0] * cos_t - moved[1] * sin_t
    imag_turn = moved[1] * cos_t + moved[0] * sin_t
    cos_j, sin_j = angle_table(2 * count, count, 2 * count)
    summed = jnp.einsum("rks,kj->rjs", real_turn, cos_j, precision=highest) - jnp.einsum(
        "rks,kj->rjs", imag_turn, sin_j, precision=highest
    )
    return summed / float(2 * count * width)


def times_spec(left, right):
    return jnp.stack(
        [left[0] * right[0] - left[1] * right[1], left[0] * right[1] + left[1] * right[0]]
    )


def times_conj(left, right):
    return jnp.stack(
        [left[0] * right[0] + left[1] * right[1], left[1] * right[0] - left[0] * right[1]]
    )


def shards(x_slab, filter_taps, mix_weight, skip_gain, cotangent):
    chans = cotangent.shape[0]
    width = cotangent.shape[1]
    count = lax.axis_size("ctx")
    piece = mix_weight
    projected = lax.psum_scatter(
        jnp.einsum("ijo,il->ojl", piece, x_slab, preferred_element_type=jnp.float32),
        "ch",
        scatter_dimension=0,
        tiled=True,
    )
    outer_gate = projected[:, 0]
    inner_gate = projected[:, 1]
    values_in = projected[:, 2]
    product = inner_gate * values_in
    grad_out = cotangent.astype(jnp.float32)
    gain = skip_gain[:, None]
    spectra_all = spectrum(spread(jnp.concatenate([product, filter_taps], 0)))
    prod_spec = spectra_all[:, :chans]
    filt_spec = spectra_all[:, chans:]
    convolved = gather_back(unspectrum(times_spec(prod_spec, filt_spec)))
    mixed = convolved + gain * product
    grad_mixed = grad_out * outer_gate
    grad_outer = grad_out * mixed
    grad_spec = spectrum(spread(grad_mixed))
    adjoint = gather_back(
        unspectrum(
            jnp.concatenate([times_conj(grad_spec, filt_spec), times_conj(grad_spec, prod_spec)], 1)
        )
    )
    grad_product = adjoint[:chans] + gain * grad_mixed
    grad_filter = adjoint[chans:]
    grad_proj = jnp.stack(
        [grad_outer, grad_product * values_in, grad_product * inner_gate], 1
    ).astype(jnp.bfloat16)
    all_grads = lax.all_gather(grad_proj, "ch", axis=0, tiled=True)
    scale = 1.0 / math.sqrt(count * width)
    piece = x_slab
    weight_grad = lax.psum_scatter(
        jnp.einsum("il,ojl->ijo", piece, all_grads, preferred_element_type=jnp.float32) * scale,
        "ctx",
        scatter_dimension=0,
        tiled=True,
    )
    input_grad = jnp.einsum(
        "ijo,ojl->il", mix_weight, all_grads, preferred_element_type=jnp.float32
    )
    return (input_grad.astype(jnp.bfloat16), weight_grad, grad_filter * scale)


MESH = pl.DeviceIdType.MESH
PER_OWNER = 4


def toeplitz(row, put):
    lanes = row.shape[1]
    keep = lax.broadcasted_iota(jnp.int32, (lanes, lanes), 1) >= lax.broadcasted_iota(
        jnp.int32, (lanes, lanes), 0
    )
    before = jnp.zeros((lanes, lanes), jnp.float32)
    for d in range(row.shape[0]):
        turned = pltpu.roll(
            jnp.broadcast_to(row[d : d + 1], (lanes, lanes)), 0, 1, stride=1, stride_axis=0
        )
        put(d, jnp.where(keep, turned, before).astype(jnp.bfloat16))
        before = turned


def shifted(block, down):
    rows = block.shape[0]
    place = lax.broadcasted_iota(jnp.int32, block.shape, 0)
    parts = []
    for d in range(rows):
        if d == 0:
            parts.append(block)
        elif down:
            parts.append(jnp.where(place >= d, pltpu.roll(block, d, 0), 0.0))
        else:
            parts.append(jnp.where(place < rows - d, pltpu.roll(block, rows - d, 0), 0.0))
    return jnp.concatenate(parts, axis=1).astype(jnp.bfloat16)


def fused(
    n, m, scale,
    x_hbm, f_ref, w_hbm, gain_ref, cot_ref,
    gx_ref, gw_ref, gf_ref,
    xv, wv, xall, cot32, fsend, fall, part, psend, precv, csum, csend, call,
    tcat, tvert, gall, gf32, gmat, fgs, fgall,
    lsem, xs, xr, fs, fr, ps, pr, cs, cr, hs, hr, gs, gr,
):
    k = lax.axis_index("ctx")
    h = lax.axis_index("ch")
    chans = f_ref.shape[0]
    width = f_ref.shape[1]
    rows = xall.shape[0]
    core_h = h + 1 - 2 * lax.rem(h, 2)
    y_h = lax.rem(h + 2, m)
    diag_h = lax.rem(core_h + 2, m)
    bf16, f32 = jnp.bfloat16, jnp.float32

    def remote(src, dst, send, recv, kk, hh):
        return pltpu.make_async_remote_copy(
            src_ref=src, dst_ref=dst, send_sem=send, recv_sem=recv,
            device_id=(kk, hh), device_id_type=MESH,
        )

    load_x = pltpu.make_async_copy(x_hbm, xv, lsem.at[0])
    load_x.start()
    load_w = [
        pltpu.make_async_copy(w_hbm.at[j], wv.at[:, pl.ds(j * 128, 128)], lsem.at[1 + j])
        for j in range(3)
    ]
    for copy in load_w:
        copy.start()
    own_x = pltpu.make_async_copy(
        x_hbm.at[pl.ds(pl.multiple_of(k * rows, rows), rows), :],
        xall.at[:, pl.ds(pl.multiple_of(k * width, width), width)],
        lsem.at[4],
    )
    own_x.start()

    barrier = pltpu.get_barrier_semaphore()
    for i in range(1, n):
        pl.semaphore_signal(barrier, 1, device_id=(lax.rem(k + i, n), h), device_id_type=MESH)
    for i in range(1, m):
        pl.semaphore_signal(barrier, 1, device_id=(k, lax.rem(h + i, m)), device_id_type=MESH)

    cot32[...] = cot_ref[...].astype(f32)
    for q in range(n):
        fsend[q, 0:4, :] = f_ref[pl.ds(q, PER_OWNER, stride=n), :]
        fsend[q, 4:8, :] = cot32[pl.ds(q, PER_OWNER, stride=n), :]
    fall[k] = fsend[k]
    pl.semaphore_wait(barrier, n + m - 2)

    sends = []
    for i in range(1, n):
        kk = lax.rem(k + i, n)
        copy = remote(fsend.at[kk], fall.at[k], fs.at[i], fr.at[k], kk, h)
        copy.start()
        sends.append(copy)
    for i in range(1, n):
        kk = lax.rem(k + i, n)
        copy = remote(
            x_hbm.at[pl.ds(pl.multiple_of(kk * rows, rows), rows), :],
            xall.at[:, pl.ds(pl.multiple_of(k * width, width), width)],
            xs.at[i], xr.at[k], kk, h,
        )
        copy.start()
        sends.append(copy)

    load_x.wait()
    for copy in load_w:
        copy.wait()
    turned = jnp.dot(xv[...].T, wv[...], preferred_element_type=f32)
    for j in range(3):
        piece = turned[:, j * 128 : (j + 1) * 128].T
        for q in range(m):
            cut = piece[q * chans : (q + 1) * chans]
            part[q, j * chans : (j + 1) * chans, :] = cut
            psend[q, j * chans : (j + 1) * chans, :] = cut.astype(bf16)
    for i in range(1, m):
        hh = lax.rem(h + i, m)
        copy = remote(psend.at[hh], precv.at[h], ps.at[i], pr.at[h], k, hh)
        copy.start()
        sends.append(copy)

    for i in range(1, n):
        kk = lax.rem(k + n - i, n)
        remote(fsend.at[kk], fall.at[kk], fs.at[i], fr.at[kk], kk, h).wait_recv()
    for c in range(PER_OWNER):
        def put_f(d, tile, c=c):
            tcat[c, 0:128, d * 128 : (d + 1) * 128] = tile
            tvert[c, d * 128 : (d + 1) * 128, :] = tile
        toeplitz(fall[:, c, :], put_f)

    total = part[h]
    for i in range(1, m):
        hh = lax.rem(h + m - i, m)
        remote(psend.at[hh], precv.at[hh], ps.at[i], pr.at[hh], k, hh).wait_recv()
        total = total + precv[hh].astype(f32)
    csum[...] = total
    for q in range(n):
        csend[q] = csum[pl.ds(q, 3 * PER_OWNER, stride=n), :]
    call[k] = csend[k]
    for i in range(1, n):
        kk = lax.rem(k + i, n)
        copy = remote(csend.at[kk], call.at[k], cs.at[i], cr.at[k], kk, h)
        copy.start()
        sends.append(copy)
    for i in range(1, n):
        kk = lax.rem(k + n - i, n)
        remote(csend.at[kk], call.at[kk], cs.at[i], cr.at[kk], kk, h).wait_recv()

    me = h * n + k
    made = []
    for c in range(PER_OWNER):
        outer = call[:, c, :]
        inner = call[:, PER_OWNER + c, :]
        value = call[:, 2 * PER_OWNER + c, :]
        grad_out = fall[:, PER_OWNER + c, :]
        gain = gain_ref[c * n + k]
        product = inner * value
        grad_mixed = grad_out * outer

        def put_p(d, tile, c=c):
            tcat[c, 128:256, d * 128 : (d + 1) * 128] = tile
        toeplitz(product, put_p)
        convolved = jnp.dot(shifted(product, True), tvert[c], preferred_element_type=f32)
        both = lax.dot_general(
            shifted(grad_mixed, False), tcat[c], (((1,), (1,)), ((), ())),
            preferred_element_type=f32,
        )
        grad_product = both[:, :128] + gain * grad_mixed
        fgs[:, c, :] = both[:, 128:] * scale
        made.append(
            (grad_out * (convolved + gain * product), grad_product * value, grad_product * inner)
        )
    for j in range(3):
        for c in range(0, PER_OWNER, 2):
            gall[me, j * chans + c * n : j * chans + (c + 2) * n, :] = jnp.concatenate(
                [made[c][j], made[c + 1][j]], axis=0
            ).astype(bf16)

    count = 0

    def push(slot, kk, hh, index):
        copy = remote(gall.at[slot], gall.at[slot], gs.at[index], gr.at[slot], kk, hh)
        copy.start()
        sends.append(copy)

    def landed(slot):
        remote(gall.at[slot], gall.at[slot], gs.at[0], gr.at[slot], k, y_h).wait_recv()

    for i in range(1, n):
        push(me, lax.rem(k + i, n), h, count)
        count += 1
    push(me, k, y_h, count)
    push(me, k, core_h, count + 1)
    count += 2
    fgall[k] = fgs[k]
    for i in range(1, n):
        kk = lax.rem(k + i, n)
        copy = remote(fgs.at[kk], fgall.at[k], hs.at[i], hr.at[k], kk, h)
        copy.start()
        sends.append(copy)
    for i in range(1, n):
        slot = h * n + lax.rem(k + n - i, n)
        landed(slot)
        push(slot, k, y_h, count)
        push(slot, k, core_h, count + 1)
        count += 2
    for i in range(n):
        slot = y_h * n + lax.rem(k + n - i, n)
        landed(slot)
        push(slot, k, core_h, count)
        count += 1
    for i in range(1, n):
        kk = lax.rem(k + n - i, n)
        remote(fgs.at[kk], fgall.at[kk], hs.at[i], hr.at[kk], kk, h).wait_recv()
    for c in range(PER_OWNER):
        gf_ref[c * n : (c + 1) * n, :] = fgall[:, c, :]
    own_x.wait()
    for i in range(1, n):
        kk = lax.rem(k + n - i, n)
        remote(
            x_hbm.at[pl.ds(pl.multiple_of(kk * rows, rows), rows), :],
            xall.at[:, pl.ds(pl.multiple_of(kk * width, width), width)],
            xs.at[i], xr.at[kk], kk, h,
        ).wait_recv()
    for i in range(n):
        for hh in (core_h, diag_h):
            landed(hh * n + lax.rem(k + n - i, n))

    block = 3 * chans
    for q in range(m * n):
        gf32[q * block : (q + 1) * block, :] = gall[q].astype(f32)
    for hh in range(m):
        for j in range(3):
            for c in range(0, PER_OWNER, 2):
                for b in range(n):
                    pair = [
                        gf32[pl.ds(hh * n * block + j * chans + cc * n + b, n, stride=block), :]
                        for cc in (c, c + 1)
                    ]
                    start = j * 128 + hh * chans + c * n
                    gmat[start : start + 2 * n, b * 128 : (b + 1) * 128] = jnp.concatenate(
                        pair, axis=0
                    ).astype(bf16)
    here = gmat[:, pl.ds(pl.multiple_of(k * width, width), width)]
    gx_ref[...] = jnp.dot(wv[...], here, preferred_element_type=f32).astype(bf16)
    wide = lax.dot_general(
        xall[...], gmat[...], (((1,), (1,)), ((), ())), preferred_element_type=f32
    ) * scale
    for j in range(3):
        gw_ref[j] = wide[:, j * 128 : (j + 1) * 128]
    for copy in sends:
        copy.wait_send()


def fused_shards(n, m, x_slab, filter_taps, mix_weight, skip_gain, cotangent):
    depth, width = x_slab.shape
    chans = cotangent.shape[0]
    rows = depth // n
    total = chans * m
    bf16, f32 = jnp.bfloat16, jnp.float32
    scale = 1.0 / math.sqrt(n * width)
    dma = pltpu.SemaphoreType.DMA
    vmem = pl.BlockSpec(memory_space=pltpu.VMEM)
    anywhere = pl.BlockSpec(memory_space=pl.ANY)
    gx, gw, gf = pl.pallas_call(
        functools.partial(fused, n, m, scale),
        out_shape=(
            jax.ShapeDtypeStruct((depth, width), bf16),
            jax.ShapeDtypeStruct((3, rows, total), f32),
            jax.ShapeDtypeStruct((chans, width), f32),
        ),
        in_specs=[anywhere, vmem, anywhere, pl.BlockSpec(memory_space=pltpu.SMEM), vmem],
        out_specs=(vmem, vmem, vmem),
        scratch_shapes=[
            pltpu.VMEM((depth, width), bf16),
            pltpu.VMEM((depth, 3 * total), bf16),
            pltpu.VMEM((rows, n * width), bf16),
            pltpu.VMEM((chans, width), f32),
            pltpu.VMEM((n, 2 * PER_OWNER, width), f32),
            pltpu.VMEM((n, 2 * PER_OWNER, width), f32),
            pltpu.VMEM((m, 3 * chans, width), f32),
            pltpu.VMEM((m, 3 * chans, width), bf16),
            pltpu.VMEM((m, 3 * chans, width), bf16),
            pltpu.VMEM((3 * chans, width), f32),
            pltpu.VMEM((n, 3 * PER_OWNER, width), f32),
            pltpu.VMEM((n, 3 * PER_OWNER, width), f32),
            pltpu.VMEM((PER_OWNER, 2 * width, n * width), bf16),
            pltpu.VMEM((PER_OWNER, n * width, width), bf16),
            pltpu.VMEM((m * n, 3 * chans, width), bf16),
            pltpu.VMEM((m * n * 3 * chans, width), f32),
            pltpu.VMEM((3 * total, n * width), bf16),
            pltpu.VMEM((n, PER_OWNER, width), f32),
            pltpu.VMEM((n, PER_OWNER, width), f32),
            dma((5,)),
            dma((n,)), dma((n,)),
            dma((n,)), dma((n,)),
            dma((m,)), dma((m,)),
            dma((n,)), dma((n,)),
            dma((n,)), dma((n,)),
            dma((n + 1 + 2 * (n - 1) + n,)), dma((m * n,)),
        ],
        compiler_params=pltpu.CompilerParams(
            collective_id=0, has_side_effects=True, vmem_limit_bytes=40 * 1024 * 1024
        ),
    )(x_slab, filter_taps, jnp.transpose(mix_weight, (1, 0, 2)), skip_gain, cotangent)
    return (gx, jnp.transpose(gw, (1, 0, 2)), gf)


def solution(mesh):
    n, m = mesh.shape["ctx"], mesh.shape["ch"]

    def body(x_slab, filter_taps, mix_weight, skip_gain, cotangent):
        chans, width = cotangent.shape
        if chans == PER_OWNER * n and width == 128 and n == 8 and m == 4:
            return fused_shards(n, m, x_slab, filter_taps, mix_weight, skip_gain, cotangent)
        return shards(x_slab, filter_taps, mix_weight, skip_gain, cotangent)

    in_specs = (P("ch", "ctx"), P("ch", "ctx"), P("ch", None, None), P("ch"), P("ch", "ctx"))
    out_specs = (P("ch", "ctx"), P(("ch", "ctx"), None, None), P("ch", "ctx"))
    return jax.shard_map(body, mesh=mesh, in_specs=in_specs, out_specs=out_specs, check_vma=False)
```

```python
import functools
import math

import jax
import jax.numpy as jnp
from jax import lax
from jax.experimental import pallas as pl
from jax.experimental.pallas import tpu as pltpu
from jax.sharding import PartitionSpec as P

highest = lax.Precision.HIGHEST


def angle_table(rows, cols, period):
    product = (
        jnp.arange(rows, dtype=jnp.int32)[:, None]
        * jnp.arange(cols, dtype=jnp.int32)[None, :]
        % period
    )
    phase = product.astype(jnp.float32) * (2.0 * math.pi / period)
    return (jnp.cos(phase), jnp.sin(phase))


def twiddle(count, width):
    span = width // count
    places = lax.axis_index("ctx") * span + jnp.arange(span, dtype=jnp.int32)
    total = 2 * count * width
    product = jnp.arange(2 * count, dtype=jnp.int32)[:, None] * places[None, :] % total
    phase = product.astype(jnp.float32) * (2.0 * math.pi / total)
    return (jnp.cos(phase), jnp.sin(phase))


def spread(fields):
    return lax.all_to_all(fields[:, None, :], "ctx", split_axis=2, concat_axis=1, tiled=True)


def gather_back(parted):
    joined = lax.all_to_all(parted, "ctx", split_axis=1, concat_axis=2, tiled=True)
    return joined[:, 0, :]


def spectrum(parted):
    count = parted.shape[1]
    width = count * parted.shape[2]
    cos_j, sin_j = angle_table(count, 2 * count, 2 * count)
    real_part = jnp.einsum("rjs,jk->rks", parted, cos_j, precision=highest)
    imag_part = -jnp.einsum("rjs,jk->rks", parted, sin_j, precision=highest)
    cos_t, sin_t = twiddle(count, width)
    turned = jnp.stack(
        [real_part * cos_t + imag_part * sin_t, imag_part * cos_t - real_part * sin_t]
    )
    moved = lax.all_to_all(turned, "ctx", split_axis=2, concat_axis=3, tiled=True)
    cos_b, sin_b = angle_table(width, width, width)
    real_out = jnp.einsum("rkb,bm->rkm", moved[0], cos_b, precision=highest) + jnp.einsum(
        "rkb,bm->rkm", moved[1], sin_b, precision=highest
    )
    imag_out = jnp.einsum("rkb,bm->rkm", moved[1], cos_b, precision=highest) - jnp.einsum(
        "rkb,bm->rkm", moved[0], sin_b, precision=highest
    )
    return jnp.stack([real_out, imag_out])


def unspectrum(spec):
    count = lax.axis_size("ctx")
    width = spec.shape[3]
    cos_b, sin_b = angle_table(width, width, width)
    real_part = jnp.einsum("rkm,mb->rkb", spec[0], cos_b, precision=highest) - jnp.einsum(
        "rkm,mb->rkb", spec[1], sin_b, precision=highest
    )
    imag_part = jnp.einsum("rkm,mb->rkb", spec[1], cos_b, precision=highest) + jnp.einsum(
        "rkm,mb->rkb", spec[0], sin_b, precision=highest
    )
    moved = lax.all_to_all(
        jnp.stack([real_part, imag_part]), "ctx", split_axis=3, concat_axis=2, tiled=True
    )
    cos_t, sin_t = twiddle(count, width)
    real_turn = moved[0] * cos_t - moved[1] * sin_t
    imag_turn = moved[1] * cos_t + moved[0] * sin_t
    cos_j, sin_j = angle_table(2 * count, count, 2 * count)
    summed = jnp.einsum("rks,kj->rjs", real_turn, cos_j, precision=highest) - jnp.einsum(
        "rks,kj->rjs", imag_turn, sin_j, precision=highest
    )
    return summed / float(2 * count * width)


def times_spec(left, right):
    return jnp.stack(
        [left[0] * right[0] - left[1] * right[1], left[0] * right[1] + left[1] * right[0]]
    )


def times_conj(left, right):
    return jnp.stack(
        [left[0] * right[0] + left[1] * right[1], left[1] * right[0] - left[0] * right[1]]
    )


def shards(x_slab, filter_taps, mix_weight, skip_gain, cotangent):
    chans = cotangent.shape[0]
    width = cotangent.shape[1]
    count = lax.axis_size("ctx")
    piece = mix_weight
    projected = lax.psum_scatter(
        jnp.einsum("ijo,il->ojl", piece, x_slab, preferred_element_type=jnp.float32),
        "ch",
        scatter_dimension=0,
        tiled=True,
    )
    outer_gate = projected[:, 0]
    inner_gate = projected[:, 1]
    values_in = projected[:, 2]
    product = inner_gate * values_in
    grad_out = cotangent.astype(jnp.float32)
    gain = skip_gain[:, None]
    spectra_all = spectrum(spread(jnp.concatenate([product, filter_taps], 0)))
    prod_spec = spectra_all[:, :chans]
    filt_spec = spectra_all[:, chans:]
    convolved = gather_back(unspectrum(times_spec(prod_spec, filt_spec)))
    mixed = convolved + gain * product
    grad_mixed = grad_out * outer_gate
    grad_outer = grad_out * mixed
    grad_spec = spectrum(spread(grad_mixed))
    adjoint = gather_back(
        unspectrum(
            jnp.concatenate([times_conj(grad_spec, filt_spec), times_conj(grad_spec, prod_spec)], 1)
        )
    )
    grad_product = adjoint[:chans] + gain * grad_mixed
    grad_filter = adjoint[chans:]
    grad_proj = jnp.stack(
        [grad_outer, grad_product * values_in, grad_product * inner_gate], 1
    ).astype(jnp.bfloat16)
    all_grads = lax.all_gather(grad_proj, "ch", axis=0, tiled=True)
    scale = 1.0 / math.sqrt(count * width)
    piece = x_slab
    weight_grad = lax.psum_scatter(
        jnp.einsum("il,ojl->ijo", piece, all_grads, preferred_element_type=jnp.float32) * scale,
        "ctx",
        scatter_dimension=0,
        tiled=True,
    )
    input_grad = jnp.einsum(
        "ijo,ojl->il", mix_weight, all_grads, preferred_element_type=jnp.float32
    )
    return (input_grad.astype(jnp.bfloat16), weight_grad, grad_filter * scale)


MESH = pl.DeviceIdType.MESH
PER_OWNER = 4
CUTS = (0, 6, 10, 16)


def toeplitz(row, put):
    lanes = row.shape[1]
    keep = lax.broadcasted_iota(jnp.int32, (lanes, lanes), 1) >= lax.broadcasted_iota(
        jnp.int32, (lanes, lanes), 0
    )
    before = jnp.zeros((lanes, lanes), jnp.float32)
    for d in range(row.shape[0]):
        turned = pltpu.roll(
            jnp.broadcast_to(row[d : d + 1], (lanes, lanes)), 0, 1, stride=1, stride_axis=0
        )
        put(d, jnp.where(keep, turned, before).astype(jnp.bfloat16))
        before = turned


def shifted(block, down):
    rows = block.shape[0]
    place = lax.broadcasted_iota(jnp.int32, block.shape, 0)
    parts = []
    for d in range(rows):
        if d == 0:
            parts.append(block)
        elif down:
            parts.append(jnp.where(place >= d, pltpu.roll(block, d, 0), 0.0))
        else:
            parts.append(jnp.where(place < rows - d, pltpu.roll(block, rows - d, 0), 0.0))
    return jnp.concatenate(parts, axis=1).astype(jnp.bfloat16)


def fused(
    n, m, scale,
    x_hbm, f_hbm, w_hbm, gain_hbm, cot_hbm,
    gmat, xall, gf_ref,
    f_ref, cot_ref, gain_ref, xv, wv, cot32, fsend, fall, part, psend, precv, csum, csend, call,
    tcat, tvert, gall, gf32, fgs, fgall,
    lsem, xs, xr, fs, fr, ps, pr, cs, cr, hs, hr, gs, gr,
):
    k = lax.axis_index("ctx")
    h = lax.axis_index("ch")
    chans = f_ref.shape[0]
    width = f_ref.shape[1]
    rows = xall.shape[0]
    cuts = [rows * c // 16 for c in CUTS]
    pieces = [(a, b - a) for a, b in zip(cuts[:-1], cuts[1:])]
    sends = []
    core_h = h + 1 - 2 * lax.rem(h, 2)
    y_h = lax.rem(h + 2, m)
    diag_h = lax.rem(core_h + 2, m)
    bf16, f32 = jnp.bfloat16, jnp.float32

    def remote(src, dst, send, recv, kk, hh):
        return pltpu.make_async_remote_copy(
            src_ref=src, dst_ref=dst, send_sem=send, recv_sem=recv,
            device_id=(kk, hh), device_id_type=MESH,
        )

    def x_copy(i, part_of, source, target):
        start, size = pieces[part_of]
        return remote(
            x_hbm.at[pl.ds(pl.multiple_of(target * rows + start, 16), size), :],
            xall.at[pl.ds(start, size), pl.ds(pl.multiple_of(source * width, width), width)],
            xs.at[part_of * n + i], xr.at[part_of * n + source], target, h,
        )

    def wait_x(i, part_of, source):
        start, size = pieces[part_of]
        block = xall.at[pl.ds(start, size), pl.ds(pl.multiple_of(source * width, width), width)]
        remote(
            block, block, xs.at[part_of * n + i], xr.at[part_of * n + source], source, h
        ).wait_recv()

    def send_x(part_of):
        for i in range(1, n):
            copy = x_copy(i, part_of, k, lax.rem(k + i, n))
            copy.start()
            sends.append(copy)

    load_x = pltpu.make_async_copy(x_hbm, xv, lsem.at[0])
    load_w = [
        pltpu.make_async_copy(w_hbm.at[j], wv.at[:, pl.ds(j * 128, 128)], lsem.at[1 + j])
        for j in range(3)
    ]
    load_small = [
        pltpu.make_async_copy(f_hbm, f_ref, lsem.at[5]),
        pltpu.make_async_copy(cot_hbm, cot_ref, lsem.at[6]),
        pltpu.make_async_copy(gain_hbm, gain_ref, lsem.at[7]),
    ]
    own_x = pltpu.make_async_copy(
        x_hbm.at[pl.ds(pl.multiple_of(k * rows, rows), rows), :],
        xall.at[:, pl.ds(pl.multiple_of(k * width, width), width)],
        lsem.at[4],
    )
    for copy in load_small + [load_x] + load_w + [own_x]:
        copy.start()

    barrier = pltpu.get_barrier_semaphore()
    for i in range(1, n):
        pl.semaphore_signal(barrier, 1, device_id=(lax.rem(k + i, n), h), device_id_type=MESH)
    for i in range(1, m):
        pl.semaphore_signal(barrier, 1, device_id=(k, lax.rem(h + i, m)), device_id_type=MESH)

    for copy in load_small:
        copy.wait()
    cot32[...] = cot_ref[...].astype(f32)
    for q in range(n):
        fsend[q, 0:4, :] = f_ref[pl.ds(q, PER_OWNER, stride=n), :]
        fsend[q, 4:8, :] = cot32[pl.ds(q, PER_OWNER, stride=n), :]
    fall[k] = fsend[k]
    pl.semaphore_wait(barrier, n + m - 2)

    for i in range(1, n):
        kk = lax.rem(k + i, n)
        copy = remote(fsend.at[kk], fall.at[k], fs.at[i], fr.at[k], kk, h)
        copy.start()
        sends.append(copy)
    send_x(0)

    load_x.wait()
    for copy in load_w:
        copy.wait()
    turned = jnp.dot(xv[...].T, wv[...], preferred_element_type=f32)
    for j in range(3):
        piece = turned[:, j * 128 : (j + 1) * 128].T
        for q in range(m):
            cut = piece[q * chans : (q + 1) * chans]
            part[q, j * chans : (j + 1) * chans, :] = cut
            psend[q, j * chans : (j + 1) * chans, :] = cut.astype(bf16)
    for i in range(1, m):
        hh = lax.rem(h + i, m)
        copy = remote(psend.at[hh], precv.at[h], ps.at[i], pr.at[h], k, hh)
        copy.start()
        sends.append(copy)

    for i in range(1, n):
        kk = lax.rem(k + n - i, n)
        remote(fsend.at[kk], fall.at[kk], fs.at[i], fr.at[kk], kk, h).wait_recv()
    for c in range(PER_OWNER):
        def put_f(d, tile, c=c):
            tcat[c, 0:128, d * 128 : (d + 1) * 128] = tile
            tvert[c, d * 128 : (d + 1) * 128, :] = tile
        toeplitz(fall[:, c, :], put_f)

    total = part[h]
    for i in range(1, m):
        hh = lax.rem(h + m - i, m)
        remote(psend.at[hh], precv.at[hh], ps.at[i], pr.at[hh], k, hh).wait_recv()
        total = total + precv[hh].astype(f32)
    csum[...] = total
    for q in range(n):
        csend[q] = csum[pl.ds(q, 3 * PER_OWNER, stride=n), :]
    call[k] = csend[k]
    for i in range(1, n):
        kk = lax.rem(k + i, n)
        copy = remote(csend.at[kk], call.at[k], cs.at[i], cr.at[k], kk, h)
        copy.start()
        sends.append(copy)
    send_x(1)
    for i in range(1, n):
        kk = lax.rem(k + n - i, n)
        remote(csend.at[kk], call.at[kk], cs.at[i], cr.at[kk], kk, h).wait_recv()

    me = h * n + k
    made = []
    for c in range(PER_OWNER):
        outer = call[:, c, :]
        inner = call[:, PER_OWNER + c, :]
        value = call[:, 2 * PER_OWNER + c, :]
        grad_out = fall[:, PER_OWNER + c, :]
        gain = gain_ref[c * n + k]
        product = inner * value
        grad_mixed = grad_out * outer

        def put_p(d, tile, c=c):
            tcat[c, 128:256, d * 128 : (d + 1) * 128] = tile
        toeplitz(product, put_p)
        convolved = jnp.dot(shifted(product, True), tvert[c], preferred_element_type=f32)
        both = lax.dot_general(
            shifted(grad_mixed, False), tcat[c], (((1,), (1,)), ((), ())),
            preferred_element_type=f32,
        )
        grad_product = both[:, :128] + gain * grad_mixed
        fgs[:, c, :] = both[:, 128:] * scale
        made.append(
            (grad_out * (convolved + gain * product), grad_product * value, grad_product * inner)
        )
    for j in range(3):
        for c in range(0, PER_OWNER, 2):
            gall[me, j * chans + c * n : j * chans + (c + 2) * n, :] = jnp.concatenate(
                [made[c][j], made[c + 1][j]], axis=0
            ).astype(bf16)

    count = 0

    def push(slot, kk, hh, index):
        copy = remote(gall.at[slot], gall.at[slot], gs.at[index], gr.at[slot], kk, hh)
        copy.start()
        sends.append(copy)

    def landed(slot):
        remote(gall.at[slot], gall.at[slot], gs.at[0], gr.at[slot], k, y_h).wait_recv()

    for i in range(1, n):
        push(me, lax.rem(k + i, n), h, count)
        count += 1
    push(me, k, y_h, count)
    push(me, k, core_h, count + 1)
    count += 2
    send_x(2)
    fgall[k] = fgs[k]
    for i in range(1, n):
        kk = lax.rem(k + i, n)
        copy = remote(fgs.at[kk], fgall.at[k], hs.at[i], hr.at[k], kk, h)
        copy.start()
        sends.append(copy)
    for i in range(1, n):
        slot = h * n + lax.rem(k + n - i, n)
        landed(slot)
        push(slot, k, y_h, count)
        push(slot, k, core_h, count + 1)
        count += 2
    for i in range(n):
        slot = y_h * n + lax.rem(k + n - i, n)
        landed(slot)
        push(slot, k, core_h, count)
        count += 1
    for i in range(1, n):
        kk = lax.rem(k + n - i, n)
        remote(fgs.at[kk], fgall.at[kk], hs.at[i], hr.at[kk], kk, h).wait_recv()
    for c in range(PER_OWNER):
        gf_ref[c * n : (c + 1) * n, :] = fgall[:, c, :]
    own_x.wait()
    for i in range(1, n):
        kk = lax.rem(k + n - i, n)
        for part_of in range(3):
            wait_x(i, part_of, kk)
    for i in range(n):
        for hh in (core_h, diag_h):
            landed(hh * n + lax.rem(k + n - i, n))

    block = 3 * chans
    for q in range(m * n):
        gf32[q * block : (q + 1) * block, :] = gall[q].astype(f32)
    for hh in range(m):
        for j in range(3):
            for c in range(0, PER_OWNER, 2):
                for b in range(n):
                    pair = [
                        gf32[pl.ds(hh * n * block + j * chans + cc * n + b, n, stride=block), :]
                        for cc in (c, c + 1)
                    ]
                    start = j * 128 + hh * chans + c * n
                    gmat[start : start + 2 * n, b * 128 : (b + 1) * 128] = jnp.concatenate(
                        pair, axis=0
                    ).astype(bf16)
    for copy in sends:
        copy.wait_send()


def finish(
    parts, scale, g_hbm, x_hbm, w_hbm, f_hbm, gx_hbm, gw_hbm, gf_hbm,
    gv, xv, wv, fv, gx, gw, lsem, wsem, osem,
):
    k = lax.axis_index("ctx")
    depth, width = gx.shape
    total = gw.shape[2]
    step = depth // parts
    load_g = pltpu.make_async_copy(g_hbm, gv, lsem.at[0])
    load_x = pltpu.make_async_copy(x_hbm, xv, lsem.at[1])
    load_f = pltpu.make_async_copy(f_hbm, fv, lsem.at[2])
    load_w = [
        pltpu.make_async_copy(
            w_hbm.at[j, pl.ds(p * step, step), :],
            wv.at[pl.ds(p * step, step), pl.ds(j * total, total)],
            wsem.at[p * 3 + j],
        )
        for p in range(parts)
        for j in range(3)
    ]
    for copy in [load_g, load_x] + load_w + [load_f]:
        copy.start()
    stores = []
    load_g.wait()
    load_x.wait()
    for j in range(3):
        gw[j] = lax.dot_general(
            xv[...], gv[j * total : (j + 1) * total, :], (((1,), (1,)), ((), ())),
            preferred_element_type=jnp.float32,
        ) * scale
        copy = pltpu.make_async_copy(gw.at[j], gw_hbm.at[j], osem.at[j])
        copy.start()
        stores.append(copy)
    here = gv[:, pl.ds(pl.multiple_of(k * width, width), width)]
    for p in range(parts):
        for j in range(3):
            load_w[p * 3 + j].wait()
        span = pl.ds(p * step, step)
        gx[span, :] = jnp.dot(wv[span, :], here, preferred_element_type=jnp.float32).astype(
            jnp.bfloat16
        )
        copy = pltpu.make_async_copy(gx.at[span, :], gx_hbm.at[span, :], osem.at[3 + p])
        copy.start()
        stores.append(copy)
    load_f.wait()
    copy = pltpu.make_async_copy(fv, gf_hbm, osem.at[3 + parts])
    copy.start()
    stores.append(copy)
    for copy in stores:
        copy.wait()


def fused_shards(n, m, x_slab, filter_taps, mix_weight, skip_gain, cotangent):
    depth, width = x_slab.shape
    chans = cotangent.shape[0]
    rows = depth // n
    total = chans * m
    bf16, f32 = jnp.bfloat16, jnp.float32
    scale = 1.0 / math.sqrt(n * width)
    dma = pltpu.SemaphoreType.DMA
    vmem = pl.BlockSpec(memory_space=pltpu.VMEM)
    hbm = pl.BlockSpec(memory_space=pltpu.HBM)
    weights = jnp.transpose(mix_weight, (1, 0, 2))
    grads, x_rows, taps = pl.pallas_call(
        functools.partial(fused, n, m, scale),
        out_shape=(
            jax.ShapeDtypeStruct((3 * total, n * width), bf16),
            jax.ShapeDtypeStruct((rows, n * width), bf16),
            jax.ShapeDtypeStruct((chans, width), f32),
        ),
        in_specs=[hbm] * 5,
        out_specs=(vmem, hbm, vmem),
        scratch_shapes=[
            pltpu.VMEM((chans, width), f32),
            pltpu.VMEM((chans, width), bf16),
            pltpu.SMEM((chans,), f32),
            pltpu.VMEM((depth, width), bf16),
            pltpu.VMEM((depth, 3 * total), bf16),
            pltpu.VMEM((chans, width), f32),
            pltpu.VMEM((n, 2 * PER_OWNER, width), f32),
            pltpu.VMEM((n, 2 * PER_OWNER, width), f32),
            pltpu.VMEM((m, 3 * chans, width), f32),
            pltpu.VMEM((m, 3 * chans, width), bf16),
            pltpu.VMEM((m, 3 * chans, width), bf16),
            pltpu.VMEM((3 * chans, width), f32),
            pltpu.VMEM((n, 3 * PER_OWNER, width), f32),
            pltpu.VMEM((n, 3 * PER_OWNER, width), f32),
            pltpu.VMEM((PER_OWNER, 2 * width, n * width), bf16),
            pltpu.VMEM((PER_OWNER, n * width, width), bf16),
            pltpu.VMEM((m * n, 3 * chans, width), bf16),
            pltpu.VMEM((m * n * 3 * chans, width), f32),
            pltpu.VMEM((n, PER_OWNER, width), f32),
            pltpu.VMEM((n, PER_OWNER, width), f32),
            dma((8,)),
            dma((3 * n,)), dma((3 * n,)),
            dma((n,)), dma((n,)),
            dma((m,)), dma((m,)),
            dma((n,)), dma((n,)),
            dma((n,)), dma((n,)),
            dma((n + 1 + 2 * (n - 1) + n,)), dma((m * n,)),
        ],
        compiler_params=pltpu.CompilerParams(
            collective_id=0, has_side_effects=True, vmem_limit_bytes=60 * 1024 * 1024
        ),
    )(x_slab, filter_taps, weights, skip_gain, cotangent)
    parts = 4
    gx, gw, gf = pl.pallas_call(
        functools.partial(finish, parts, scale),
        out_shape=(
            jax.ShapeDtypeStruct((depth, width), bf16),
            jax.ShapeDtypeStruct((3, rows, total), f32),
            jax.ShapeDtypeStruct((chans, width), f32),
        ),
        in_specs=[hbm] * 4,
        out_specs=(hbm, hbm, hbm),
        scratch_shapes=[
            pltpu.VMEM((3 * total, n * width), bf16),
            pltpu.VMEM((rows, n * width), bf16),
            pltpu.VMEM((depth, 3 * total), bf16),
            pltpu.VMEM((chans, width), f32),
            pltpu.VMEM((depth, width), bf16),
            pltpu.VMEM((3, rows, total), f32),
            dma((3,)), dma((3 * parts,)), dma((4 + parts,)),
        ],
        compiler_params=pltpu.CompilerParams(vmem_limit_bytes=60 * 1024 * 1024),
    )(grads, x_rows, weights, taps)
    return (gx, jnp.transpose(gw, (1, 0, 2)), gf)


def solution(mesh):
    n, m = mesh.shape["ctx"], mesh.shape["ch"]

    def body(x_slab, filter_taps, mix_weight, skip_gain, cotangent):
        chans, width = cotangent.shape
        if chans == PER_OWNER * n and width == 128 and n == 8 and m == 4:
            return fused_shards(n, m, x_slab, filter_taps, mix_weight, skip_gain, cotangent)
        return shards(x_slab, filter_taps, mix_weight, skip_gain, cotangent)

    in_specs = (P("ch", "ctx"), P("ch", "ctx"), P("ch", None, None), P("ch"), P("ch", "ctx"))
    out_specs = (P("ch", "ctx"), P(("ch", "ctx"), None, None), P("ch", "ctx"))
    return jax.shard_map(body, mesh=mesh, in_specs=in_specs, out_specs=out_specs, check_vma=False)
```

```python
import functools
import math

import jax
import jax.numpy as jnp
from jax import lax
from jax.experimental import pallas as pl
from jax.experimental.pallas import tpu as pltpu
from jax.sharding import PartitionSpec as P

highest = lax.Precision.HIGHEST


def angle_table(rows, cols, period):
    product = (
        jnp.arange(rows, dtype=jnp.int32)[:, None]
        * jnp.arange(cols, dtype=jnp.int32)[None, :]
        % period
    )
    phase = product.astype(jnp.float32) * (2.0 * math.pi / period)
    return (jnp.cos(phase), jnp.sin(phase))


def twiddle(count, width):
    span = width // count
    places = lax.axis_index("ctx") * span + jnp.arange(span, dtype=jnp.int32)
    total = 2 * count * width
    product = jnp.arange(2 * count, dtype=jnp.int32)[:, None] * places[None, :] % total
    phase = product.astype(jnp.float32) * (2.0 * math.pi / total)
    return (jnp.cos(phase), jnp.sin(phase))


def spread(fields):
    return lax.all_to_all(fields[:, None, :], "ctx", split_axis=2, concat_axis=1, tiled=True)


def gather_back(parted):
    joined = lax.all_to_all(parted, "ctx", split_axis=1, concat_axis=2, tiled=True)
    return joined[:, 0, :]


def spectrum(parted):
    count = parted.shape[1]
    width = count * parted.shape[2]
    cos_j, sin_j = angle_table(count, 2 * count, 2 * count)
    real_part = jnp.einsum("rjs,jk->rks", parted, cos_j, precision=highest)
    imag_part = -jnp.einsum("rjs,jk->rks", parted, sin_j, precision=highest)
    cos_t, sin_t = twiddle(count, width)
    turned = jnp.stack(
        [real_part * cos_t + imag_part * sin_t, imag_part * cos_t - real_part * sin_t]
    )
    moved = lax.all_to_all(turned, "ctx", split_axis=2, concat_axis=3, tiled=True)
    cos_b, sin_b = angle_table(width, width, width)
    real_out = jnp.einsum("rkb,bm->rkm", moved[0], cos_b, precision=highest) + jnp.einsum(
        "rkb,bm->rkm", moved[1], sin_b, precision=highest
    )
    imag_out = jnp.einsum("rkb,bm->rkm", moved[1], cos_b, precision=highest) - jnp.einsum(
        "rkb,bm->rkm", moved[0], sin_b, precision=highest
    )
    return jnp.stack([real_out, imag_out])


def unspectrum(spec):
    count = lax.axis_size("ctx")
    width = spec.shape[3]
    cos_b, sin_b = angle_table(width, width, width)
    real_part = jnp.einsum("rkm,mb->rkb", spec[0], cos_b, precision=highest) - jnp.einsum(
        "rkm,mb->rkb", spec[1], sin_b, precision=highest
    )
    imag_part = jnp.einsum("rkm,mb->rkb", spec[1], cos_b, precision=highest) + jnp.einsum(
        "rkm,mb->rkb", spec[0], sin_b, precision=highest
    )
    moved = lax.all_to_all(
        jnp.stack([real_part, imag_part]), "ctx", split_axis=3, concat_axis=2, tiled=True
    )
    cos_t, sin_t = twiddle(count, width)
    real_turn = moved[0] * cos_t - moved[1] * sin_t
    imag_turn = moved[1] * cos_t + moved[0] * sin_t
    cos_j, sin_j = angle_table(2 * count, count, 2 * count)
    summed = jnp.einsum("rks,kj->rjs", real_turn, cos_j, precision=highest) - jnp.einsum(
        "rks,kj->rjs", imag_turn, sin_j, precision=highest
    )
    return summed / float(2 * count * width)


def times_spec(left, right):
    return jnp.stack(
        [left[0] * right[0] - left[1] * right[1], left[0] * right[1] + left[1] * right[0]]
    )


def times_conj(left, right):
    return jnp.stack(
        [left[0] * right[0] + left[1] * right[1], left[1] * right[0] - left[0] * right[1]]
    )


def shards(x_slab, filter_taps, mix_weight, skip_gain, cotangent):
    chans = cotangent.shape[0]
    width = cotangent.shape[1]
    count = lax.axis_size("ctx")
    piece = mix_weight
    projected = lax.psum_scatter(
        jnp.einsum("ijo,il->ojl", piece, x_slab, preferred_element_type=jnp.float32),
        "ch",
        scatter_dimension=0,
        tiled=True,
    )
    outer_gate = projected[:, 0]
    inner_gate = projected[:, 1]
    values_in = projected[:, 2]
    product = inner_gate * values_in
    grad_out = cotangent.astype(jnp.float32)
    gain = skip_gain[:, None]
    spectra_all = spectrum(spread(jnp.concatenate([product, filter_taps], 0)))
    prod_spec = spectra_all[:, :chans]
    filt_spec = spectra_all[:, chans:]
    convolved = gather_back(unspectrum(times_spec(prod_spec, filt_spec)))
    mixed = convolved + gain * product
    grad_mixed = grad_out * outer_gate
    grad_outer = grad_out * mixed
    grad_spec = spectrum(spread(grad_mixed))
    adjoint = gather_back(
        unspectrum(
            jnp.concatenate([times_conj(grad_spec, filt_spec), times_conj(grad_spec, prod_spec)], 1)
        )
    )
    grad_product = adjoint[:chans] + gain * grad_mixed
    grad_filter = adjoint[chans:]
    grad_proj = jnp.stack(
        [grad_outer, grad_product * values_in, grad_product * inner_gate], 1
    ).astype(jnp.bfloat16)
    all_grads = lax.all_gather(grad_proj, "ch", axis=0, tiled=True)
    scale = 1.0 / math.sqrt(count * width)
    piece = x_slab
    weight_grad = lax.psum_scatter(
        jnp.einsum("il,ojl->ijo", piece, all_grads, preferred_element_type=jnp.float32) * scale,
        "ctx",
        scatter_dimension=0,
        tiled=True,
    )
    input_grad = jnp.einsum(
        "ijo,ojl->il", mix_weight, all_grads, preferred_element_type=jnp.float32
    )
    return (input_grad.astype(jnp.bfloat16), weight_grad, grad_filter * scale)


MESH = pl.DeviceIdType.MESH
PER_OWNER = 4
CUTS = (0, 5, 9, 16)


def toeplitz(row, put):
    lanes = row.shape[1]
    keep = lax.broadcasted_iota(jnp.int32, (lanes, lanes), 1) >= lax.broadcasted_iota(
        jnp.int32, (lanes, lanes), 0
    )
    before = jnp.zeros((lanes, lanes), jnp.float32)
    for d in range(row.shape[0]):
        turned = pltpu.roll(
            jnp.broadcast_to(row[d : d + 1], (lanes, lanes)), 0, 1, stride=1, stride_axis=0
        )
        put(d, jnp.where(keep, turned, before).astype(jnp.bfloat16))
        before = turned


def shifted(block, down):
    rows = block.shape[0]
    place = lax.broadcasted_iota(jnp.int32, block.shape, 0)
    parts = []
    for d in range(rows):
        if d == 0:
            parts.append(block)
        elif down:
            parts.append(jnp.where(place >= d, pltpu.roll(block, d, 0), 0.0))
        else:
            parts.append(jnp.where(place < rows - d, pltpu.roll(block, rows - d, 0), 0.0))
    return jnp.concatenate(parts, axis=1).astype(jnp.bfloat16)


def fused(
    n, m, scale,
    x_hbm, f_hbm, w_hbm, gain_hbm, cot_hbm,
    g_hbm, xall, gf_ref,
    f_ref, cot_ref, gain_ref, xv, wv, cot32, fsend, fall, part, psend, precv, csum, csend, call,
    tcat, tvert, gall, gf32, gmat, fgs, fgall,
    osem, lsem, xs, xr, fs, fr, ps, pr, cs, cr, hs, hr, gs, gr,
):
    k = lax.axis_index("ctx")
    h = lax.axis_index("ch")
    chans = f_ref.shape[0]
    width = f_ref.shape[1]
    rows = xall.shape[0]
    cuts = [rows * c // 16 for c in CUTS]
    pieces = [(a, b - a) for a, b in zip(cuts[:-1], cuts[1:])]
    sends = []
    core_h = h + 1 - 2 * lax.rem(h, 2)
    y_h = lax.rem(h + 2, m)
    diag_h = lax.rem(core_h + 2, m)
    bf16, f32 = jnp.bfloat16, jnp.float32

    def remote(src, dst, send, recv, kk, hh):
        return pltpu.make_async_remote_copy(
            src_ref=src, dst_ref=dst, send_sem=send, recv_sem=recv,
            device_id=(kk, hh), device_id_type=MESH,
        )

    def x_copy(i, part_of, source, target):
        start, size = pieces[part_of]
        return remote(
            x_hbm.at[pl.ds(pl.multiple_of(target * rows + start, 16), size), :],
            xall.at[pl.ds(start, size), pl.ds(pl.multiple_of(source * width, width), width)],
            xs.at[part_of * n + i], xr.at[part_of * n + source], target, h,
        )

    def wait_x(i, part_of, source):
        start, size = pieces[part_of]
        block = xall.at[pl.ds(start, size), pl.ds(pl.multiple_of(source * width, width), width)]
        remote(
            block, block, xs.at[part_of * n + i], xr.at[part_of * n + source], source, h
        ).wait_recv()

    def send_x(part_of):
        for i in range(1, n):
            copy = x_copy(i, part_of, k, lax.rem(k + i, n))
            copy.start()
            sends.append(copy)

    load_x = pltpu.make_async_copy(x_hbm, xv, lsem.at[0])
    load_w = [
        pltpu.make_async_copy(w_hbm.at[j], wv.at[:, pl.ds(j * 128, 128)], lsem.at[1 + j])
        for j in range(3)
    ]
    load_small = [
        pltpu.make_async_copy(f_hbm, f_ref, lsem.at[5]),
        pltpu.make_async_copy(cot_hbm, cot_ref, lsem.at[6]),
        pltpu.make_async_copy(gain_hbm, gain_ref, lsem.at[7]),
    ]
    own_x = pltpu.make_async_copy(
        x_hbm.at[pl.ds(pl.multiple_of(k * rows, rows), rows), :],
        xall.at[:, pl.ds(pl.multiple_of(k * width, width), width)],
        lsem.at[4],
    )
    for copy in load_small + [load_x] + load_w + [own_x]:
        copy.start()

    barrier = pltpu.get_barrier_semaphore()
    for i in range(1, n):
        pl.semaphore_signal(barrier, 1, device_id=(lax.rem(k + i, n), h), device_id_type=MESH)
    for i in range(1, m):
        pl.semaphore_signal(barrier, 1, device_id=(k, lax.rem(h + i, m)), device_id_type=MESH)

    for copy in load_small:
        copy.wait()
    cot32[...] = cot_ref[...].astype(f32)
    for q in range(n):
        fsend[q, 0:4, :] = f_ref[pl.ds(q, PER_OWNER, stride=n), :]
        fsend[q, 4:8, :] = cot32[pl.ds(q, PER_OWNER, stride=n), :]
    fall[k] = fsend[k]
    load_x.wait()
    for copy in load_w:
        copy.wait()
    turned = jnp.dot(xv[...].T, wv[...], preferred_element_type=f32)
    for j in range(3):
        piece = turned[:, j * 128 : (j + 1) * 128].T
        for q in range(m):
            cut = piece[q * chans : (q + 1) * chans]
            part[q, j * chans : (j + 1) * chans, :] = cut
            psend[q, j * chans : (j + 1) * chans, :] = cut.astype(bf16)
    pl.semaphore_wait(barrier, n + m - 2)
    for i in range(1, m):
        hh = lax.rem(h + i, m)
        copy = remote(psend.at[hh], precv.at[h], ps.at[i], pr.at[h], k, hh)
        copy.start()
        sends.append(copy)
    for i in range(1, n):
        kk = lax.rem(k + i, n)
        copy = remote(fsend.at[kk], fall.at[k], fs.at[i], fr.at[k], kk, h)
        copy.start()
        sends.append(copy)
    send_x(0)


    for i in range(1, n):
        kk = lax.rem(k + n - i, n)
        remote(fsend.at[kk], fall.at[kk], fs.at[i], fr.at[kk], kk, h).wait_recv()
    for c in range(PER_OWNER):
        def put_f(d, tile, c=c):
            tcat[c, 0:128, d * 128 : (d + 1) * 128] = tile
            tvert[c, d * 128 : (d + 1) * 128, :] = tile
        toeplitz(fall[:, c, :], put_f)

    total = part[h]
    for i in range(1, m):
        hh = lax.rem(h + m - i, m)
        remote(psend.at[hh], precv.at[hh], ps.at[i], pr.at[hh], k, hh).wait_recv()
        total = total + precv[hh].astype(f32)
    csum[...] = total
    for q in range(n):
        csend[q] = csum[pl.ds(q, 3 * PER_OWNER, stride=n), :]
    call[k] = csend[k]
    for i in range(1, n):
        kk = lax.rem(k + i, n)
        copy = remote(csend.at[kk], call.at[k], cs.at[i], cr.at[k], kk, h)
        copy.start()
        sends.append(copy)
    send_x(1)
    for i in range(1, n):
        kk = lax.rem(k + n - i, n)
        remote(csend.at[kk], call.at[kk], cs.at[i], cr.at[kk], kk, h).wait_recv()

    me = h * n + k
    made = []
    for c in range(PER_OWNER):
        outer = call[:, c, :]
        inner = call[:, PER_OWNER + c, :]
        value = call[:, 2 * PER_OWNER + c, :]
        grad_out = fall[:, PER_OWNER + c, :]
        gain = gain_ref[c * n + k]
        product = inner * value
        grad_mixed = grad_out * outer

        def put_p(d, tile, c=c):
            tcat[c, 128:256, d * 128 : (d + 1) * 128] = tile
        toeplitz(product, put_p)
        convolved = jnp.dot(shifted(product, True), tvert[c], preferred_element_type=f32)
        both = lax.dot_general(
            shifted(grad_mixed, False), tcat[c], (((1,), (1,)), ((), ())),
            preferred_element_type=f32,
        )
        grad_product = both[:, :128] + gain * grad_mixed
        fgs[:, c, :] = both[:, 128:] * scale
        made.append(
            (grad_out * (convolved + gain * product), grad_product * value, grad_product * inner)
        )
    for j in range(3):
        for c in range(0, PER_OWNER, 2):
            gall[me, j * chans + c * n : j * chans + (c + 2) * n, :] = jnp.concatenate(
                [made[c][j], made[c + 1][j]], axis=0
            ).astype(bf16)

    block = 3 * chans
    stores = []

    def expand(place, hh):
        base = place * n * block
        for q in range(n):
            gf32[base + q * block : base + (q + 1) * block, :] = gall[hh * n + q].astype(f32)
        for j in range(3):
            for c in range(0, PER_OWNER, 2):
                start = pl.multiple_of(j * m * chans + hh * chans + c * n, 2 * n)
                for b in range(n):
                    pair = [
                        gf32[pl.ds(base + j * chans + cc * n + b, n, stride=block), :]
                        for cc in (c, c + 1)
                    ]
                    gmat[pl.ds(start, 2 * n), b * 128 : (b + 1) * 128] = jnp.concatenate(
                        pair, axis=0
                    ).astype(bf16)
            span = pl.ds(pl.multiple_of(j * m * chans + hh * chans, chans), chans)
            copy = pltpu.make_async_copy(
                gmat.at[span, :], g_hbm.at[span, :], osem.at[place * 3 + j]
            )
            copy.start()
            stores.append(copy)

    count = 0

    def push(slot, kk, hh, index):
        copy = remote(gall.at[slot], gall.at[slot], gs.at[index], gr.at[slot], kk, hh)
        copy.start()
        sends.append(copy)

    def landed(slot):
        remote(gall.at[slot], gall.at[slot], gs.at[0], gr.at[slot], k, y_h).wait_recv()

    for i in range(1, n):
        push(me, lax.rem(k + i, n), h, count)
        count += 1
    push(me, k, y_h, count)
    push(me, k, core_h, count + 1)
    count += 2
    send_x(2)
    fgall[k] = fgs[k]
    for i in range(1, n):
        kk = lax.rem(k + i, n)
        copy = remote(fgs.at[kk], fgall.at[k], hs.at[i], hr.at[k], kk, h)
        copy.start()
        sends.append(copy)
    for i in range(1, n):
        slot = h * n + lax.rem(k + n - i, n)
        landed(slot)
        push(slot, k, y_h, count)
        push(slot, k, core_h, count + 1)
        count += 2
    expand(0, h)
    for i in range(n):
        slot = y_h * n + lax.rem(k + n - i, n)
        landed(slot)
        push(slot, k, core_h, count)
        count += 1
    expand(1, y_h)
    for i in range(1, n):
        kk = lax.rem(k + n - i, n)
        remote(fgs.at[kk], fgall.at[kk], hs.at[i], hr.at[kk], kk, h).wait_recv()
    for c in range(PER_OWNER):
        gf_ref[c * n : (c + 1) * n, :] = fgall[:, c, :]
    own_x.wait()
    for i in range(1, n):
        kk = lax.rem(k + n - i, n)
        for part_of in range(3):
            wait_x(i, part_of, kk)
    for i in range(n):
        for hh in (core_h, diag_h):
            landed(hh * n + lax.rem(k + n - i, n))

    expand(2, core_h)
    expand(3, diag_h)
    for copy in stores:
        copy.wait()
    for copy in sends:
        copy.wait_send()


def finish(
    parts, scale, g_hbm, x_hbm, w_hbm, f_hbm, gx_hbm, gw_hbm, gf_hbm,
    gv, xv, wv, fv, gx, gw, lsem, wsem, osem,
):
    k = lax.axis_index("ctx")
    depth, width = gx.shape
    total = gw.shape[2]
    step = depth // parts
    load_g = pltpu.make_async_copy(g_hbm, gv, lsem.at[0])
    load_x = pltpu.make_async_copy(x_hbm, xv, lsem.at[1])
    load_f = pltpu.make_async_copy(f_hbm, fv, lsem.at[2])
    load_w = [
        pltpu.make_async_copy(
            w_hbm.at[j, pl.ds(p * step, step), :],
            wv.at[pl.ds(p * step, step), pl.ds(j * total, total)],
            wsem.at[p * 3 + j],
        )
        for p in range(parts)
        for j in range(3)
    ]
    for copy in [load_g, load_x] + load_w + [load_f]:
        copy.start()
    stores = []
    load_g.wait()
    load_x.wait()
    for j in range(3):
        gw[j] = lax.dot_general(
            xv[...], gv[j * total : (j + 1) * total, :], (((1,), (1,)), ((), ())),
            preferred_element_type=jnp.float32,
        ) * scale
        copy = pltpu.make_async_copy(gw.at[j], gw_hbm.at[j], osem.at[j])
        copy.start()
        stores.append(copy)
    here = gv[:, pl.ds(pl.multiple_of(k * width, width), width)]
    for p in range(parts):
        for j in range(3):
            load_w[p * 3 + j].wait()
        span = pl.ds(p * step, step)
        gx[span, :] = jnp.dot(wv[span, :], here, preferred_element_type=jnp.float32).astype(
            jnp.bfloat16
        )
        copy = pltpu.make_async_copy(gx.at[span, :], gx_hbm.at[span, :], osem.at[3 + p])
        copy.start()
        stores.append(copy)
    load_f.wait()
    copy = pltpu.make_async_copy(fv, gf_hbm, osem.at[3 + parts])
    copy.start()
    stores.append(copy)
    for copy in stores:
        copy.wait()


def fused_shards(n, m, x_slab, filter_taps, mix_weight, skip_gain, cotangent):
    depth, width = x_slab.shape
    chans = cotangent.shape[0]
    rows = depth // n
    total = chans * m
    bf16, f32 = jnp.bfloat16, jnp.float32
    scale = 1.0 / math.sqrt(n * width)
    dma = pltpu.SemaphoreType.DMA
    vmem = pl.BlockSpec(memory_space=pltpu.VMEM)
    hbm = pl.BlockSpec(memory_space=pltpu.HBM)
    weights = jnp.transpose(mix_weight, (1, 0, 2))
    grads, x_rows, taps = pl.pallas_call(
        functools.partial(fused, n, m, scale),
        out_shape=(
            jax.ShapeDtypeStruct((3 * total, n * width), bf16),
            jax.ShapeDtypeStruct((rows, n * width), bf16),
            jax.ShapeDtypeStruct((chans, width), f32),
        ),
        in_specs=[hbm] * 5,
        out_specs=(hbm, hbm, vmem),
        scratch_shapes=[
            pltpu.VMEM((chans, width), f32),
            pltpu.VMEM((chans, width), bf16),
            pltpu.SMEM((chans,), f32),
            pltpu.VMEM((depth, width), bf16),
            pltpu.VMEM((depth, 3 * total), bf16),
            pltpu.VMEM((chans, width), f32),
            pltpu.VMEM((n, 2 * PER_OWNER, width), f32),
            pltpu.VMEM((n, 2 * PER_OWNER, width), f32),
            pltpu.VMEM((m, 3 * chans, width), f32),
            pltpu.VMEM((m, 3 * chans, width), bf16),
            pltpu.VMEM((m, 3 * chans, width), bf16),
            pltpu.VMEM((3 * chans, width), f32),
            pltpu.VMEM((n, 3 * PER_OWNER, width), f32),
            pltpu.VMEM((n, 3 * PER_OWNER, width), f32),
            pltpu.VMEM((PER_OWNER, 2 * width, n * width), bf16),
            pltpu.VMEM((PER_OWNER, n * width, width), bf16),
            pltpu.VMEM((m * n, 3 * chans, width), bf16),
            pltpu.VMEM((m * n * 3 * chans, width), f32),
            pltpu.VMEM((3 * total, n * width), bf16),
            pltpu.VMEM((n, PER_OWNER, width), f32),
            pltpu.VMEM((n, PER_OWNER, width), f32),
            dma((3 * m,)),
            dma((8,)),
            dma((3 * n,)), dma((3 * n,)),
            dma((n,)), dma((n,)),
            dma((m,)), dma((m,)),
            dma((n,)), dma((n,)),
            dma((n,)), dma((n,)),
            dma((n + 1 + 2 * (n - 1) + n,)), dma((m * n,)),
        ],
        compiler_params=pltpu.CompilerParams(
            collective_id=0, has_side_effects=True, vmem_limit_bytes=60 * 1024 * 1024
        ),
    )(x_slab, filter_taps, weights, skip_gain, cotangent)
    parts = 4
    gx, gw, gf = pl.pallas_call(
        functools.partial(finish, parts, scale),
        out_shape=(
            jax.ShapeDtypeStruct((depth, width), bf16),
            jax.ShapeDtypeStruct((3, rows, total), f32),
            jax.ShapeDtypeStruct((chans, width), f32),
        ),
        in_specs=[hbm] * 4,
        out_specs=(hbm, hbm, hbm),
        scratch_shapes=[
            pltpu.VMEM((3 * total, n * width), bf16),
            pltpu.VMEM((rows, n * width), bf16),
            pltpu.VMEM((depth, 3 * total), bf16),
            pltpu.VMEM((chans, width), f32),
            pltpu.VMEM((depth, width), bf16),
            pltpu.VMEM((3, rows, total), f32),
            dma((3,)), dma((3 * parts,)), dma((4 + parts,)),
        ],
        compiler_params=pltpu.CompilerParams(vmem_limit_bytes=60 * 1024 * 1024),
    )(grads, x_rows, weights, taps)
    return (gx, jnp.transpose(gw, (1, 0, 2)), gf)


def solution(mesh):
    n, m = mesh.shape["ctx"], mesh.shape["ch"]

    def body(x_slab, filter_taps, mix_weight, skip_gain, cotangent):
        chans, width = cotangent.shape
        if chans == PER_OWNER * n and width == 128 and n == 8 and m == 4:
            return fused_shards(n, m, x_slab, filter_taps, mix_weight, skip_gain, cotangent)
        return shards(x_slab, filter_taps, mix_weight, skip_gain, cotangent)

    in_specs = (P("ch", "ctx"), P("ch", "ctx"), P("ch", None, None), P("ch"), P("ch", "ctx"))
    out_specs = (P("ch", "ctx"), P(("ch", "ctx"), None, None), P("ch", "ctx"))
    return jax.shard_map(body, mesh=mesh, in_specs=in_specs, out_specs=out_specs, check_vma=False)
```

```python
import functools
import math

import jax
import jax.numpy as jnp
from jax import lax
from jax.experimental import pallas as pl
from jax.experimental.pallas import tpu as pltpu
from jax.sharding import PartitionSpec as P

highest = lax.Precision.HIGHEST


def angle_table(rows, cols, period):
    product = (
        jnp.arange(rows, dtype=jnp.int32)[:, None]
        * jnp.arange(cols, dtype=jnp.int32)[None, :]
        % period
    )
    phase = product.astype(jnp.float32) * (2.0 * math.pi / period)
    return (jnp.cos(phase), jnp.sin(phase))


def twiddle(count, width):
    span = width // count
    places = lax.axis_index("ctx") * span + jnp.arange(span, dtype=jnp.int32)
    total = 2 * count * width
    product = jnp.arange(2 * count, dtype=jnp.int32)[:, None] * places[None, :] % total
    phase = product.astype(jnp.float32) * (2.0 * math.pi / total)
    return (jnp.cos(phase), jnp.sin(phase))


def spread(fields):
    return lax.all_to_all(fields[:, None, :], "ctx", split_axis=2, concat_axis=1, tiled=True)


def gather_back(parted):
    joined = lax.all_to_all(parted, "ctx", split_axis=1, concat_axis=2, tiled=True)
    return joined[:, 0, :]


def spectrum(parted):
    count = parted.shape[1]
    width = count * parted.shape[2]
    cos_j, sin_j = angle_table(count, 2 * count, 2 * count)
    real_part = jnp.einsum("rjs,jk->rks", parted, cos_j, precision=highest)
    imag_part = -jnp.einsum("rjs,jk->rks", parted, sin_j, precision=highest)
    cos_t, sin_t = twiddle(count, width)
    turned = jnp.stack(
        [real_part * cos_t + imag_part * sin_t, imag_part * cos_t - real_part * sin_t]
    )
    moved = lax.all_to_all(turned, "ctx", split_axis=2, concat_axis=3, tiled=True)
    cos_b, sin_b = angle_table(width, width, width)
    real_out = jnp.einsum("rkb,bm->rkm", moved[0], cos_b, precision=highest) + jnp.einsum(
        "rkb,bm->rkm", moved[1], sin_b, precision=highest
    )
    imag_out = jnp.einsum("rkb,bm->rkm", moved[1], cos_b, precision=highest) - jnp.einsum(
        "rkb,bm->rkm", moved[0], sin_b, precision=highest
    )
    return jnp.stack([real_out, imag_out])


def unspectrum(spec):
    count = lax.axis_size("ctx")
    width = spec.shape[3]
    cos_b, sin_b = angle_table(width, width, width)
    real_part = jnp.einsum("rkm,mb->rkb", spec[0], cos_b, precision=highest) - jnp.einsum(
        "rkm,mb->rkb", spec[1], sin_b, precision=highest
    )
    imag_part = jnp.einsum("rkm,mb->rkb", spec[1], cos_b, precision=highest) + jnp.einsum(
        "rkm,mb->rkb", spec[0], sin_b, precision=highest
    )
    moved = lax.all_to_all(
        jnp.stack([real_part, imag_part]), "ctx", split_axis=3, concat_axis=2, tiled=True
    )
    cos_t, sin_t = twiddle(count, width)
    real_turn = moved[0] * cos_t - moved[1] * sin_t
    imag_turn = moved[1] * cos_t + moved[0] * sin_t
    cos_j, sin_j = angle_table(2 * count, count, 2 * count)
    summed = jnp.einsum("rks,kj->rjs", real_turn, cos_j, precision=highest) - jnp.einsum(
        "rks,kj->rjs", imag_turn, sin_j, precision=highest
    )
    return summed / float(2 * count * width)


def times_spec(left, right):
    return jnp.stack(
        [left[0] * right[0] - left[1] * right[1], left[0] * right[1] + left[1] * right[0]]
    )


def times_conj(left, right):
    return jnp.stack(
        [left[0] * right[0] + left[1] * right[1], left[1] * right[0] - left[0] * right[1]]
    )


def shards(x_slab, filter_taps, mix_weight, skip_gain, cotangent):
    chans = cotangent.shape[0]
    width = cotangent.shape[1]
    count = lax.axis_size("ctx")
    piece = mix_weight
    projected = lax.psum_scatter(
        jnp.einsum("ijo,il->ojl", piece, x_slab, preferred_element_type=jnp.float32),
        "ch",
        scatter_dimension=0,
        tiled=True,
    )
    outer_gate = projected[:, 0]
    inner_gate = projected[:, 1]
    values_in = projected[:, 2]
    product = inner_gate * values_in
    grad_out = cotangent.astype(jnp.float32)
    gain = skip_gain[:, None]
    spectra_all = spectrum(spread(jnp.concatenate([product, filter_taps], 0)))
    prod_spec = spectra_all[:, :chans]
    filt_spec = spectra_all[:, chans:]
    convolved = gather_back(unspectrum(times_spec(prod_spec, filt_spec)))
    mixed = convolved + gain * product
    grad_mixed = grad_out * outer_gate
    grad_outer = grad_out * mixed
    grad_spec = spectrum(spread(grad_mixed))
    adjoint = gather_back(
        unspectrum(
            jnp.concatenate([times_conj(grad_spec, filt_spec), times_conj(grad_spec, prod_spec)], 1)
        )
    )
    grad_product = adjoint[:chans] + gain * grad_mixed
    grad_filter = adjoint[chans:]
    grad_proj = jnp.stack(
        [grad_outer, grad_product * values_in, grad_product * inner_gate], 1
    ).astype(jnp.bfloat16)
    all_grads = lax.all_gather(grad_proj, "ch", axis=0, tiled=True)
    scale = 1.0 / math.sqrt(count * width)
    piece = x_slab
    weight_grad = lax.psum_scatter(
        jnp.einsum("il,ojl->ijo", piece, all_grads, preferred_element_type=jnp.float32) * scale,
        "ctx",
        scatter_dimension=0,
        tiled=True,
    )
    input_grad = jnp.einsum(
        "ijo,ojl->il", mix_weight, all_grads, preferred_element_type=jnp.float32
    )
    return (input_grad.astype(jnp.bfloat16), weight_grad, grad_filter * scale)


MESH = pl.DeviceIdType.MESH
PER_OWNER = 4
CUTS = (0, 5, 9, 16)


def toeplitz(row, put):
    lanes = row.shape[1]
    keep = lax.broadcasted_iota(jnp.int32, (lanes, lanes), 1) >= lax.broadcasted_iota(
        jnp.int32, (lanes, lanes), 0
    )
    before = jnp.zeros((lanes, lanes), jnp.float32)
    for d in range(row.shape[0]):
        turned = pltpu.roll(
            jnp.broadcast_to(row[d : d + 1], (lanes, lanes)), 0, 1, stride=1, stride_axis=0
        )
        put(d, jnp.where(keep, turned, before).astype(jnp.bfloat16))
        before = turned


def shifted(block, down):
    rows = block.shape[0]
    place = lax.broadcasted_iota(jnp.int32, block.shape, 0)
    parts = []
    for d in range(rows):
        if d == 0:
            parts.append(block)
        elif down:
            parts.append(jnp.where(place >= d, pltpu.roll(block, d, 0), 0.0))
        else:
            parts.append(jnp.where(place < rows - d, pltpu.roll(block, rows - d, 0), 0.0))
    return jnp.concatenate(parts, axis=1).astype(jnp.bfloat16)


def fused(
    n, m, scale,
    x_hbm, f_hbm, w_hbm, gain_hbm, cot_hbm,
    g_hbm, xall, gf_ref,
    f_ref, cot_ref, gain_ref, xv, wv, cot32, fsend, fall, part, psend, precv, csum, csend, call,
    tcat, tvert, gall, gf32, gmat, fgs, fgall,
    osem, lsem, xs, xr, fs, fr, ps, pr, cs, cr, hs, hr, gs, gr,
):
    k = lax.axis_index("ctx")
    h = lax.axis_index("ch")
    chans = f_ref.shape[0]
    width = f_ref.shape[1]
    rows = xall.shape[0]
    cuts = [rows * c // 16 for c in CUTS]
    pieces = [(a, b - a) for a, b in zip(cuts[:-1], cuts[1:])]
    sends = []
    core_h = h + 1 - 2 * lax.rem(h, 2)
    y_h = lax.rem(h + 2, m)
    diag_h = lax.rem(core_h + 2, m)
    bf16, f32 = jnp.bfloat16, jnp.float32

    def remote(src, dst, send, recv, kk, hh):
        return pltpu.make_async_remote_copy(
            src_ref=src, dst_ref=dst, send_sem=send, recv_sem=recv,
            device_id=(kk, hh), device_id_type=MESH,
        )

    def x_copy(i, part_of, source, target):
        start, size = pieces[part_of]
        return remote(
            x_hbm.at[pl.ds(pl.multiple_of(target * rows + start, 16), size), :],
            xall.at[pl.ds(start, size), pl.ds(pl.multiple_of(source * width, width), width)],
            xs.at[part_of * n + i], xr.at[part_of * n + source], target, h,
        )

    def wait_x(i, part_of, source):
        start, size = pieces[part_of]
        block = xall.at[pl.ds(start, size), pl.ds(pl.multiple_of(source * width, width), width)]
        remote(
            block, block, xs.at[part_of * n + i], xr.at[part_of * n + source], source, h
        ).wait_recv()

    def send_x(part_of):
        for i in range(1, n):
            copy = x_copy(i, part_of, k, lax.rem(k + i, n))
            copy.start()
            sends.append(copy)

    load_x = pltpu.make_async_copy(x_hbm, xv, lsem.at[0])
    load_w = [
        pltpu.make_async_copy(w_hbm.at[j], wv.at[:, pl.ds(j * 128, 128)], lsem.at[1 + j])
        for j in range(3)
    ]
    load_small = [
        pltpu.make_async_copy(f_hbm, f_ref, lsem.at[5]),
        pltpu.make_async_copy(cot_hbm, cot_ref, lsem.at[6]),
        pltpu.make_async_copy(gain_hbm, gain_ref, lsem.at[7]),
    ]
    own_x = pltpu.make_async_copy(
        x_hbm.at[pl.ds(pl.multiple_of(k * rows, rows), rows), :],
        xall.at[:, pl.ds(pl.multiple_of(k * width, width), width)],
        lsem.at[4],
    )
    for copy in load_small + [load_x] + load_w + [own_x]:
        copy.start()

    barrier = pltpu.get_barrier_semaphore()
    for i in range(1, n):
        pl.semaphore_signal(barrier, 1, device_id=(lax.rem(k + i, n), h), device_id_type=MESH)
    for i in range(1, m):
        pl.semaphore_signal(barrier, 1, device_id=(k, lax.rem(h + i, m)), device_id_type=MESH)

    for copy in load_small:
        copy.wait()
    cot32[...] = cot_ref[...].astype(f32)
    for q in range(n):
        fsend[q, 0:4, :] = f_ref[pl.ds(q, PER_OWNER, stride=n), :]
        fsend[q, 4:8, :] = cot32[pl.ds(q, PER_OWNER, stride=n), :]
    fall[k] = fsend[k]
    load_x.wait()
    for copy in load_w:
        copy.wait()
    turned = jnp.dot(xv[...].T, wv[...], preferred_element_type=f32)
    for j in range(3):
        piece = turned[:, j * 128 : (j + 1) * 128].T
        for q in range(m):
            cut = piece[q * chans : (q + 1) * chans]
            part[q, j * chans : (j + 1) * chans, :] = cut
            psend[q, j * chans : (j + 1) * chans, :] = cut.astype(bf16)
    pl.semaphore_wait(barrier, n + m - 2)
    for i in range(1, m):
        hh = lax.rem(h + i, m)
        copy = remote(psend.at[hh], precv.at[h], ps.at[i], pr.at[h], k, hh)
        copy.start()
        sends.append(copy)
    for i in range(1, n):
        kk = lax.rem(k + i, n)
        copy = remote(fsend.at[kk], fall.at[k], fs.at[i], fr.at[k], kk, h)
        copy.start()
        sends.append(copy)
    send_x(0)


    for i in range(1, n):
        kk = lax.rem(k + n - i, n)
        remote(fsend.at[kk], fall.at[kk], fs.at[i], fr.at[kk], kk, h).wait_recv()
    for c in range(PER_OWNER):
        def put_f(d, tile, c=c):
            tcat[c, 0:128, d * 128 : (d + 1) * 128] = tile
            tvert[c, d * 128 : (d + 1) * 128, :] = tile
        toeplitz(fall[:, c, :], put_f)

    total = part[h]
    for i in range(1, m):
        hh = lax.rem(h + m - i, m)
        remote(psend.at[hh], precv.at[hh], ps.at[i], pr.at[hh], k, hh).wait_recv()
        total = total + precv[hh].astype(f32)
    csum[...] = total
    for q in range(n):
        csend[q] = csum[pl.ds(q, 3 * PER_OWNER, stride=n), :]
    call[k] = csend[k]
    for i in range(1, n):
        kk = lax.rem(k + i, n)
        copy = remote(csend.at[kk], call.at[k], cs.at[i], cr.at[k], kk, h)
        copy.start()
        sends.append(copy)
    send_x(1)
    for i in range(1, n):
        kk = lax.rem(k + n - i, n)
        remote(csend.at[kk], call.at[kk], cs.at[i], cr.at[kk], kk, h).wait_recv()

    me = h * n + k
    made = []
    for c in range(PER_OWNER):
        outer = call[:, c, :]
        inner = call[:, PER_OWNER + c, :]
        value = call[:, 2 * PER_OWNER + c, :]
        grad_out = fall[:, PER_OWNER + c, :]
        gain = gain_ref[c * n + k]
        product = inner * value
        grad_mixed = grad_out * outer

        def put_p(d, tile, c=c):
            tcat[c, 128:256, d * 128 : (d + 1) * 128] = tile
        toeplitz(product, put_p)
        convolved = jnp.dot(shifted(product, True), tvert[c], preferred_element_type=f32)
        both = lax.dot_general(
            shifted(grad_mixed, False), tcat[c], (((1,), (1,)), ((), ())),
            preferred_element_type=f32,
        )
        grad_product = both[:, :128] + gain * grad_mixed
        fgs[:, c, :] = both[:, 128:] * scale
        made.append(
            (grad_out * (convolved + gain * product), grad_product * value, grad_product * inner)
        )
    for j in range(3):
        for c in range(0, PER_OWNER, 2):
            gall[me, j * chans + c * n : j * chans + (c + 2) * n, :] = jnp.concatenate(
                [made[c][j], made[c + 1][j]], axis=0
            ).astype(bf16)

    block = 3 * chans
    stores = []

    def expand(place, hh):
        base = place * n * block
        for q in range(n):
            gf32[base + q * block : base + (q + 1) * block, :] = gall[hh * n + q].astype(f32)
        for j in range(3):
            for c in range(0, PER_OWNER, 2):
                start = pl.multiple_of(j * m * chans + hh * chans + c * n, 2 * n)
                for b in range(n):
                    pair = [
                        gf32[pl.ds(base + j * chans + cc * n + b, n, stride=block), :]
                        for cc in (c, c + 1)
                    ]
                    gmat[pl.ds(start, 2 * n), b * 128 : (b + 1) * 128] = jnp.concatenate(
                        pair, axis=0
                    ).astype(bf16)
            span = pl.ds(pl.multiple_of(j * m * chans + hh * chans, chans), chans)
            copy = pltpu.make_async_copy(
                gmat.at[span, :], g_hbm.at[span, :], osem.at[place * 3 + j]
            )
            copy.start()
            stores.append(copy)

    count = 0

    def push(slot, kk, hh, index):
        copy = remote(gall.at[slot], gall.at[slot], gs.at[index], gr.at[slot], kk, hh)
        copy.start()
        sends.append(copy)

    def landed(slot):
        remote(gall.at[slot], gall.at[slot], gs.at[0], gr.at[slot], k, y_h).wait_recv()

    for i in range(1, n):
        push(me, lax.rem(k + i, n), h, count)
        count += 1
    push(me, k, y_h, count)
    push(me, k, core_h, count + 1)
    count += 2
    send_x(2)
    fgall[k] = fgs[k]
    for i in range(1, n):
        kk = lax.rem(k + i, n)
        copy = remote(fgs.at[kk], fgall.at[k], hs.at[i], hr.at[k], kk, h)
        copy.start()
        sends.append(copy)
    for i in range(1, n):
        slot = h * n + lax.rem(k + n - i, n)
        landed(slot)
        push(slot, k, y_h, count)
        push(slot, k, core_h, count + 1)
        count += 2
    expand(0, h)
    for i in range(n):
        slot = y_h * n + lax.rem(k + n - i, n)
        landed(slot)
        push(slot, k, core_h, count)
        count += 1
    expand(1, y_h)
    for i in range(1, n):
        kk = lax.rem(k + n - i, n)
        remote(fgs.at[kk], fgall.at[kk], hs.at[i], hr.at[kk], kk, h).wait_recv()
    for c in range(PER_OWNER):
        gf_ref[c * n : (c + 1) * n, :] = fgall[:, c, :]
    own_x.wait()
    for i in range(1, n):
        kk = lax.rem(k + n - i, n)
        for part_of in range(3):
            wait_x(i, part_of, kk)
    for i in range(n):
        for hh in (core_h, diag_h):
            landed(hh * n + lax.rem(k + n - i, n))

    expand(2, core_h)
    expand(3, diag_h)
    for copy in stores:
        copy.wait()
    for copy in sends:
        copy.wait_send()


def finish(
    parts, scale, g_hbm, x_hbm, w_hbm, f_hbm, gx_hbm, gw_hbm, gf_hbm,
    gv, xv, wv, fv, gx, gw, lsem, wsem, osem,
):
    k = lax.axis_index("ctx")
    depth, width = gx.shape
    total = gw.shape[2]
    step = depth // parts
    load_g = pltpu.make_async_copy(g_hbm, gv, lsem.at[0])
    load_x = pltpu.make_async_copy(x_hbm, xv, lsem.at[1])
    load_f = pltpu.make_async_copy(f_hbm, fv, lsem.at[2])
    load_w = [
        pltpu.make_async_copy(
            w_hbm.at[j, pl.ds(p * step, step), :],
            wv.at[pl.ds(p * step, step), pl.ds(j * total, total)],
            wsem.at[p * 3 + j],
        )
        for p in range(parts)
        for j in range(3)
    ]
    for copy in [load_g, load_x] + load_w + [load_f]:
        copy.start()
    stores = []
    load_g.wait()
    load_x.wait()
    for j in range(3):
        gw[j] = lax.dot_general(
            xv[...], gv[j * total : (j + 1) * total, :], (((1,), (1,)), ((), ())),
            preferred_element_type=jnp.float32,
        ) * scale
        copy = pltpu.make_async_copy(gw.at[j], gw_hbm.at[j], osem.at[j])
        copy.start()
        stores.append(copy)
    here = gv[:, pl.ds(pl.multiple_of(k * width, width), width)]
    for p in range(parts):
        for j in range(3):
            load_w[p * 3 + j].wait()
        span = pl.ds(p * step, step)
        gx[span, :] = jnp.dot(wv[span, :], here, preferred_element_type=jnp.float32).astype(
            jnp.bfloat16
        )
        copy = pltpu.make_async_copy(gx.at[span, :], gx_hbm.at[span, :], osem.at[3 + p])
        copy.start()
        stores.append(copy)
    load_f.wait()
    copy = pltpu.make_async_copy(fv, gf_hbm, osem.at[3 + parts])
    copy.start()
    stores.append(copy)
    for copy in stores:
        copy.wait()


def fused_shards(n, m, x_slab, filter_taps, mix_weight, skip_gain, cotangent):
    depth, width = x_slab.shape
    chans = cotangent.shape[0]
    rows = depth // n
    total = chans * m
    bf16, f32 = jnp.bfloat16, jnp.float32
    scale = 1.0 / math.sqrt(n * width)
    dma = pltpu.SemaphoreType.DMA
    vmem = pl.BlockSpec(memory_space=pltpu.VMEM)
    hbm = pl.BlockSpec(memory_space=pltpu.HBM)
    weights = jnp.transpose(mix_weight, (1, 0, 2))
    grads, x_rows, taps = pl.pallas_call(
        functools.partial(fused, n, m, scale),
        out_shape=(
            jax.ShapeDtypeStruct((3 * total, n * width), bf16),
            jax.ShapeDtypeStruct((rows, n * width), bf16),
            jax.ShapeDtypeStruct((chans, width), f32),
        ),
        in_specs=[hbm] * 5,
        out_specs=(hbm, hbm, vmem),
        scratch_shapes=[
            pltpu.VMEM((chans, width), f32),
            pltpu.VMEM((chans, width), bf16),
            pltpu.SMEM((chans,), f32),
            pltpu.VMEM((depth, width), bf16),
            pltpu.VMEM((depth, 3 * total), bf16),
            pltpu.VMEM((chans, width), f32),
            pltpu.VMEM((n, 2 * PER_OWNER, width), f32),
            pltpu.VMEM((n, 2 * PER_OWNER, width), f32),
            pltpu.VMEM((m, 3 * chans, width), f32),
            pltpu.VMEM((m, 3 * chans, width), bf16),
            pltpu.VMEM((m, 3 * chans, width), bf16),
            pltpu.VMEM((3 * chans, width), f32),
            pltpu.VMEM((n, 3 * PER_OWNER, width), f32),
            pltpu.VMEM((n, 3 * PER_OWNER, width), f32),
            pltpu.VMEM((PER_OWNER, 2 * width, n * width), bf16),
            pltpu.VMEM((PER_OWNER, n * width, width), bf16),
            pltpu.VMEM((m * n, 3 * chans, width), bf16),
            pltpu.VMEM((m * n * 3 * chans, width), f32),
            pltpu.VMEM((3 * total, n * width), bf16),
            pltpu.VMEM((n, PER_OWNER, width), f32),
            pltpu.VMEM((n, PER_OWNER, width), f32),
            dma((3 * m,)),
            dma((8,)),
            dma((3 * n,)), dma((3 * n,)),
            dma((n,)), dma((n,)),
            dma((m,)), dma((m,)),
            dma((n,)), dma((n,)),
            dma((n,)), dma((n,)),
            dma((n + 1 + 2 * (n - 1) + n,)), dma((m * n,)),
        ],
        compiler_params=pltpu.CompilerParams(
            collective_id=0, has_side_effects=True, vmem_limit_bytes=60 * 1024 * 1024
        ),
    )(x_slab, filter_taps, weights, skip_gain, cotangent)
    parts = 2
    gx, gw, gf = pl.pallas_call(
        functools.partial(finish, parts, scale),
        out_shape=(
            jax.ShapeDtypeStruct((depth, width), bf16),
            jax.ShapeDtypeStruct((3, rows, total), f32),
            jax.ShapeDtypeStruct((chans, width), f32),
        ),
        in_specs=[hbm] * 4,
        out_specs=(hbm, hbm, hbm),
        scratch_shapes=[
            pltpu.VMEM((3 * total, n * width), bf16),
            pltpu.VMEM((rows, n * width), bf16),
            pltpu.VMEM((depth, 3 * total), bf16),
            pltpu.VMEM((chans, width), f32),
            pltpu.VMEM((depth, width), bf16),
            pltpu.VMEM((3, rows, total), f32),
            dma((3,)), dma((3 * parts,)), dma((4 + parts,)),
        ],
        compiler_params=pltpu.CompilerParams(vmem_limit_bytes=60 * 1024 * 1024),
    )(grads, x_rows, weights, taps)
    return (gx, jnp.transpose(gw, (1, 0, 2)), gf)


def solution(mesh):
    n, m = mesh.shape["ctx"], mesh.shape["ch"]

    def body(x_slab, filter_taps, mix_weight, skip_gain, cotangent):
        chans, width = cotangent.shape
        if chans == PER_OWNER * n and width == 128 and n == 8 and m == 4:
            return fused_shards(n, m, x_slab, filter_taps, mix_weight, skip_gain, cotangent)
        return shards(x_slab, filter_taps, mix_weight, skip_gain, cotangent)

    in_specs = (P("ch", "ctx"), P("ch", "ctx"), P("ch", None, None), P("ch"), P("ch", "ctx"))
    out_specs = (P("ch", "ctx"), P(("ch", "ctx"), None, None), P("ch", "ctx"))
    return jax.shard_map(body, mesh=mesh, in_specs=in_specs, out_specs=out_specs, check_vma=False)
```
